128 devices in a mesh: tm: 16 (over x, z), space: 8 (over y, core).
Axes of the slice: x: 4, y: 4, z: 4, core: 2. Of those that a mesh axis runs over, the one named last changes fastest.
Arguments:
- tokens: bfloat16 [131072, 2240], P(('tm', 'space')), may hold values from -256 to 256
- norm_gain: float32 [2240], replicated, may hold values from 0.1 to 1.9
- w_qkv: bfloat16 [2240, 3456], P(None, 'tm'), may hold values from -0.125 to 0.125
- w_out: bfloat16 [1152, 2240], P('tm'), may hold values from -0.1875 to 0.1875
- ffn_cached: bfloat16 [131072, 2240], P(('tm', 'space')), may hold values from -3 to 3
Outputs:
- mixed: bfloat16 [131072, 2240], P(('tm', 'space'))
The draws below stay inside these ranges and needn't reach their ends.
All inputs are finite; a program needn't handle non-finite values.
Results may differ from the reference program's by a relative error of at most 0.0039.
Values may be sent and summed in bfloat16 or wider, within the bound.
No kernel may reach another device: no remote copies, remote signals or barrier semaphores. Data moves between devices by JAX's collectives and lax.ppermute only.
A program may use at most 128 MiB of HBM per device.

```python
import math
import jax
import jax.numpy as jnp
from jax import lax

D = 2240
H = 36
HS = 32
TOK_DEV = 1024
SLAB = 8192
TOKENS = 131072
N_TM = 16


def draw_tokens(key, part):
    key = jax.random.fold_in(key, 11)
    key_noise, key_block, key_common, key_rows, key_columns = jax.random.split(key, 5)
    blocks = TOKENS // TOK_DEV
    jitter = jax.random.truncated_normal(key_noise, -3.0, 3.0, (TOKENS, D), jnp.float32)
    block_mean = jax.random.truncated_normal(key_block, -3.0, 3.0, (blocks, D), jnp.float32)
    common = 0.7 * jax.random.truncated_normal(key_common, -3.0, 3.0, (1, D), jnp.float32)
    row_scale = jnp.exp(jax.random.uniform(key_rows, (TOKENS, 1), jnp.float32, 0.0, math.log(10.0)))
    column_scale = jnp.exp(jax.random.uniform(key_columns, (1, D), jnp.float32, math.log(0.3), math.log(3.0)))
    spread_mean = jnp.repeat(block_mean, TOK_DEV, axis=0)
    floats = row_scale * column_scale * (common + spread_mean + jitter)
    return floats.astype(jnp.bfloat16)


def levels(rng, extent, cuts, low, high):
    def one(axis_at, shards_of):
        heights = jax.random.uniform(jax.random.fold_in(jax.random.fold_in(rng, 6), axis_at), (shards_of,), jnp.float32, low / len(cuts), high / len(cuts))
        return jnp.repeat(jnp.exp(heights), extent[axis_at] // shards_of).reshape((-1,) + (1,) * (len(extent) - axis_at - 1))

    level = one(*cuts[0])
    for cut in cuts[1:]:
        level = level * one(*cut)
    return level


def centred(rng, extent, deviation, limit, pieces=(), kind=jnp.bfloat16):
    entries = jax.random.normal(rng, extent, jnp.float32) * deviation
    if len(pieces) > 0:
        entries = levels(rng, extent, pieces, -0.22, 0.18) * entries
    return jnp.clip(entries, min=-limit, max=limit).astype(kind)


def setup_inputs(seed: int = 0) -> dict:
    keys = jax.random.split(jax.random.key(seed), 6)
    tokens = draw_tokens(jax.random.fold_in(keys[5], 71), 0)
    norm_gain = jnp.clip(1.0 + 0.18 * jax.random.normal(keys[1], (D,), jnp.float32), 0.1, 1.9)
    w_qkv = centred(keys[2], (D, 3 * H * HS), D ** -0.5, 0.125, ((1, 16),))
    w_out = centred(keys[3], (H * HS, D), (H * HS) ** -0.5, 0.1875, ((0, 16),))
    ffn_cached = centred(keys[4], (TOKENS, D), 0.5, 3.0, ((0, 128),))
    return dict(tokens=tokens, norm_gain=norm_gain, w_qkv=w_qkv, w_out=w_out, ffn_cached=ffn_cached)


def reference(tokens, norm_gain, w_qkv, w_out, ffn_cached):
    inner = H * HS
    token_slabs = tokens.reshape(N_TM, SLAB, D)
    ffn_slabs = ffn_cached.reshape(N_TM, SLAB, D)

    def advance(running, inputs):
        seen_state, seen_norm = running
        floats_in, ffn_part = inputs
        floats = floats_in.astype(jnp.float32)
        root_mean = jnp.sqrt(lax.optimization_barrier(jnp.mean(floats * floats, axis=1, keepdims=True)) + 1e-06)
        normed = (floats / root_mean * norm_gain).astype(jnp.bfloat16)
        projected = jnp.dot(normed, w_qkv, preferred_element_type=jnp.float32)
        feat_q = jax.nn.relu(projected[:, :inner]).astype(jnp.bfloat16)
        feat_k = jax.nn.relu(projected[:, inner:2 * inner]).astype(jnp.bfloat16)
        values = projected[:, 2 * inner:].astype(jnp.bfloat16)
        keys_f = feat_k.astype(jnp.float32).reshape(SLAB, H, HS)
        values_f = values.astype(jnp.float32).reshape(SLAB, H, HS)
        block_state = jnp.einsum('thi,thj->ihj', keys_f, values_f, precision=lax.Precision.HIGHEST).reshape(HS, inner)
        block_norm = lax.optimization_barrier(jnp.sum(feat_k.astype(jnp.float32), axis=0, keepdims=True))
        seen_state = seen_state + block_state
        seen_norm = seen_norm + block_norm
        queries_f = feat_q.astype(jnp.float32).reshape(SLAB, H, HS)
        numerator = jnp.einsum('thi,ihj->thj', queries_f, seen_state.reshape(HS, H, HS), precision=lax.Precision.HIGHEST)
        denominator = jnp.einsum('thi,hi->th', queries_f, seen_norm.reshape(H, HS), precision=lax.Precision.HIGHEST) + 1e-06
        attended = (numerator / denominator[:, :, None]).reshape(SLAB, inner).astype(jnp.bfloat16)
        result = jnp.dot(attended, w_out, preferred_element_type=jnp.float32) + ffn_part.astype(jnp.float32)
        return ((seen_state, seen_norm), result.astype(jnp.bfloat16))
    start_state = (jnp.zeros((HS, inner), jnp.float32), jnp.zeros((1, inner), jnp.float32))
    _, mixed = lax.scan(advance, start_state, (token_slabs, ffn_slabs))
    return mixed.reshape(TOKENS, D)
```

```python
import jax
import jax.numpy as jnp
import numpy as np
from jax import lax
from jax.experimental import pallas as pl
from jax.experimental.pallas import tpu as pltpu
from jax.sharding import PartitionSpec as P

H = 36
HS = 32
INNER = H * HS
GROUPS = INNER // 128
THIRD = 72
BOTH = ("tm", "space")
F32 = jnp.float32
BF16 = jnp.bfloat16

FIRST = {2: 6, 3: 7, 4: 8, 1: 9, 0: 10}
SECOND = {0: 12, 1: 13, 2: 14, 3: 15, 4: 11}


def device(t, y, c):
    return t * 8 + y * 2 + c


def trade_pairs():
    pairs = []
    for y in range(4):
        for d in range(5):
            a, b = FIRST[d], SECOND[d]
            pairs += [
                (device(d, y, 0), device(a, y, 0)),
                (device(a, y, 0), device(d, y, 0)),
                (device(d, y, 1), device(b, y, 0)),
                (device(b, y, 1), device(d, y, 1)),
            ]
    return pairs


def kv_third(t, c):
    if t <= 4:
        return 3 * (FIRST, SECOND)[c][t]
    return 3 * t + 1 + c


def q_third(t):
    if t <= 5:
        return 3 * t
    for d in range(5):
        if FIRST[d] == t:
            return 3 * d + 1
        if SECOND[d] == t:
            return 3 * d + 2


def along(core_axes):
    groups = {}
    for t in range(16):
        x, z = divmod(t, 4)
        for y in range(4):
            for c in range(2):
                fixed = z if core_axes[c] == "x" else x
                groups.setdefault((y, c, fixed), []).append(device(t, y, c))
    return list(groups.values())


def gather(part):
    part = lax.all_gather(part, BOTH, axis=0, tiled=True, axis_index_groups=along("zx"))
    return lax.all_gather(part, BOTH, axis=0, tiled=True, axis_index_groups=along("xz"))


def other_core(a):
    return lax.ppermute(a, "space", [(i, i ^ 1) for i in range(8)])


def state_kernel(k_ref, v_ref, out_ref):
    keys = jnp.maximum(k_ref[...], 0)
    contract = (((1,), (1,)), ((), ()))
    full = lax.dot_general(keys, v_ref[...], contract, preferred_element_type=F32)
    head = lax.broadcasted_iota(jnp.int32, (HS, 128), 1) // HS
    state = full[:HS]
    for b in range(1, 4):
        state = jnp.where(head == b, full[b * HS : (b + 1) * HS], state)
    out_ref[0, :HS, :] = state
    out_ref[0, HS:, :] = lax.dot_general(
        jnp.ones((8, keys.shape[1]), BF16), keys, contract, preferred_element_type=F32
    )


def block_states(keys, values):
    rows = keys.shape[1]
    spec = pl.BlockSpec((128, rows), lambda g: (g, 0))
    return pl.pallas_call(
        state_kernel,
        grid=(GROUPS,),
        in_specs=[spec, spec],
        out_specs=pl.BlockSpec((1, HS + 8, 128), lambda g: (g, 0, 0)),
        out_shape=jax.ShapeDtypeStruct((GROUPS, HS + 8, 128), F32),
        compiler_params=pltpu.CompilerParams(vmem_limit_bytes=32 * 2**20),
        cost_estimate=pl.CostEstimate(flops=2 * 128 * INNER * rows, bytes_accessed=4 * INNER * rows, transcendentals=0),
    )(keys, values)


def split_dot(a, b):
    total = None
    for _ in range(3):
        high = a.astype(BF16)
        part = jnp.dot(high, b, preferred_element_type=F32)
        total = part if total is None else total + part
        a = a - high.astype(F32)
    return total


def attend_kernel(q_ref, seen_ref, out_ref):
    queries = jnp.maximum(q_ref[...], 0)
    row = lax.broadcasted_iota(jnp.int32, (128, 128), 0) // HS
    column = lax.broadcasted_iota(jnp.int32, (128, 128), 1) // HS
    same = row == column
    state = jnp.where(same, jnp.concatenate([seen_ref[0, :HS, :]] * 4, axis=0), 0.0)
    norm = jnp.where(same, jnp.broadcast_to(seen_ref[0, HS : HS + 1, :], (128, 128)), 0.0)
    numerator = split_dot(state.T, queries)
    denominator = split_dot(norm, queries) + 1e-06
    out_ref[...] = (numerator / denominator).astype(BF16)


def attend(queries, seen):
    rows = queries.shape[1]
    return pl.pallas_call(
        attend_kernel,
        grid=(GROUPS,),
        in_specs=[
            pl.BlockSpec((128, rows), lambda g: (g, 0)),
            pl.BlockSpec((1, HS + 8, 128), lambda g: (g, 0, 0)),
        ],
        out_specs=pl.BlockSpec((128, rows), lambda g: (g, 0)),
        out_shape=jax.ShapeDtypeStruct((INNER, rows), BF16),
        compiler_params=pltpu.CompilerParams(vmem_limit_bytes=32 * 2**20),
        cost_estimate=pl.CostEstimate(flops=12 * 128 * INNER * rows, bytes_accessed=4 * INNER * rows, transcendentals=0),
    )(queries, seen)


def sync(state, core):
    keep = lax.dynamic_slice_in_dim(state, 4 * core, 5, 0)
    give = lax.dynamic_slice_in_dim(state, 4 * (1 - core), 5, 0)
    keep = keep + other_core(give)
    for bit in (2, 4):
        keep = keep + lax.ppermute(keep, "space", [(i, i ^ bit) for i in range(8)])
    for step in (1, 2, 4, 8):
        keep = keep + lax.ppermute(keep, "tm", [(t, t + step) for t in range(16 - step)])
    theirs = other_core(keep)
    low = jnp.where(core == 0, keep, theirs)
    high = jnp.where(core == 0, theirs, keep)
    return jnp.concatenate([low, high[1:]], axis=0)


def body(tokens, norm_gain, w_qkv, w_out, ffn_cached):
    t = lax.axis_index("tm")
    core = lax.rem(lax.axis_index("space"), 2)
    rows = tokens.shape[0]
    weights = w_qkv.T
    local = lambda j: lax.dynamic_slice_in_dim(weights, THIRD * j, THIRD, 0)

    given = local(jnp.where(t <= 4, 1 + core, 0))
    traded = lax.ppermute(given, BOTH, trade_pairs())
    part_kv = jnp.where(t <= 4, traded, local(1 + core))
    part_qo = jnp.where(core == 0, jnp.where(t >= 6, traded, weights[:THIRD]), w_out)

    floats = tokens.T.astype(F32)
    root_mean = jnp.sqrt(jnp.mean(floats * floats, axis=0, keepdims=True) + 1e-06)
    normed = (floats / root_mean * norm_gain[:, None]).astype(BF16)

    mine_kv = gather(part_kv)
    theirs_kv = other_core(mine_kv)
    project = lambda w: jnp.dot(w, normed, preferred_element_type=F32).astype(BF16)
    mine, theirs = project(mine_kv), project(theirs_kv)
    slots = (
        jnp.where(core == 0, mine, theirs).reshape(4, 4, THIRD, rows),
        jnp.where(core == 0, theirs, mine).reshape(4, 4, THIRD, rows),
    )
    thirds = {}
    for s in range(16):
        x, z = divmod(s, 4)
        thirds[kv_third(s, 0)] = slots[0][x, z]
        thirds[kv_third(s, 1)] = slots[1][z, x]
    keys = jnp.concatenate([thirds[u] for u in range(16, 32)], axis=0)
    values = jnp.concatenate([thirds[u] for u in range(32, 48)], axis=0)
    state = block_states(keys, values)

    part_qo, _ = lax.optimization_barrier((part_qo, mine_kv))
    mine_qo = gather(part_qo)
    theirs_qo = other_core(mine_qo)
    w_q = jnp.where(core == 0, mine_qo, theirs_qo)
    w_o = jnp.where(core == 0, theirs_qo, mine_qo).reshape(4, 4, THIRD, -1)
    w_o = w_o.transpose(1, 0, 2, 3).reshape(INNER, -1)
    projected = project(w_q).reshape(16, THIRD, rows)
    order = {q_third(s): s for s in range(16)}
    queries = jnp.concatenate([projected[order[u]] for u in range(16)], axis=0)

    seen = sync(state, core)
    attended = attend(queries, seen)
    branch_out = lax.dot_general(w_o, attended, (((0,), (0,)), ((), ())), preferred_element_type=F32)
    return (branch_out + ffn_cached.T.astype(F32)).astype(BF16).T


def solution(mesh):
    return jax.shard_map(
        body,
        mesh=mesh,
        in_specs=(
            P(("tm", "space"), None),
            P(),
            P(None, "tm"),
            P("tm", None),
            P(("tm", "space"), None),
        ),
        out_specs=P(("tm", "space"), None),
        check_vma=False,
    )
```

```python
import jax
import jax.numpy as jnp
from jax import lax
from jax.experimental import pallas as pl
from jax.experimental.pallas import tpu as pltpu
from jax.sharding import PartitionSpec as P

H = 36
HS = 32
INNER = H * HS
GROUPS = INNER // 128
THIRD = 72
BLOCK = 4 * THIRD
STATE_ROWS = 320
BOTH = ("tm", "space")
F32 = jnp.float32
BF16 = jnp.bfloat16

FIRST = {2: 6, 3: 7, 4: 8, 1: 9, 0: 10}
SECOND = {0: 12, 1: 13, 2: 14, 3: 15, 4: 11}


def device(x, z, y, c):
    return ((x % 4) * 4 + z % 4) * 8 + y * 2 + c


def everywhere(move):
    pairs = []
    for t in range(16):
        x, z = divmod(t, 4)
        for y in range(4):
            for c in range(2):
                pairs.append((device(x, z, y, c), device(*move(x, z, y, c))))
    return pairs


def trade_pairs():
    pairs = []
    at = lambda t, y, c: t * 8 + y * 2 + c
    for y in range(4):
        for d in range(5):
            a, b = FIRST[d], SECOND[d]
            pairs += [
                (at(d, y, 0), at(a, y, 0)),
                (at(a, y, 0), at(d, y, 0)),
                (at(d, y, 1), at(b, y, 0)),
                (at(b, y, 1), at(d, y, 1)),
            ]
    return pairs


def kv_third(t, c):
    if t <= 4:
        return 3 * (FIRST, SECOND)[c][t]
    return 3 * t + 1 + c


KV_AT = {kv_third(t, c): (t // 4, t % 4, c) for t in range(16) for c in range(2)}


def q_third(t):
    if t <= 5:
        return 3 * t
    for d in range(5):
        if FIRST[d] == t:
            return 3 * d + 1
        if SECOND[d] == t:
            return 3 * d + 2


Q_AT = {q_third(t): t for t in range(16)}


def pieces(group):
    row, end, out = 128 * group, 128 * group + 128, []
    while row < end:
        third = row // THIRD
        stop = min(end, THIRD * (third + 1))
        out.append((third, row - THIRD * third, stop - THIRD * third))
        row = stop
    return out


def send(a, move):
    return lax.ppermute(a, BOTH, everywhere(move))


def first_axis(step):
    return lambda x, z, y, c: (x, z + step, y, c) if c == 0 else (x + step, z, y, c)


def second_axis(step):
    return lambda x, z, y, c: (x + step, z, y, c) if c == 0 else (x, z + step, y, c)


def other_core(a):
    return send(a, lambda x, z, y, c: (x, z, y, 1 - c))


def along(core_axes):
    groups = {}
    for t in range(16):
        x, z = divmod(t, 4)
        for y in range(4):
            for c in range(2):
                fixed = z if core_axes[c] == "x" else x
                groups.setdefault((y, c, fixed), []).append(device(x, z, y, c))
    return list(groups.values())


def project_kernel(count, *refs):
    weights, normed_ref, out_ref = refs[:count], refs[count], refs[-1]
    step = pl.program_id(0)
    for n in range(count):

        @pl.when(step == n)
        def _():
            out = jnp.dot(weights[n][...], normed_ref[...], preferred_element_type=F32)
            out_ref[0] = out.astype(BF16).astype(F32)


def project(buffer, normed, blocks):
    places = list(blocks)
    count = len(places)
    depth, rows = normed.shape

    def place(n):
        out = jnp.int32(places[-1])
        for i in range(count - 1):
            out = jnp.where(n == i, places[i], out)
        return out

    kept = [] if buffer is None else [buffer]
    return pl.pallas_call(
        lambda *refs: project_kernel(count, *refs[: count + 1], refs[-1]),
        grid=(count,),
        in_specs=[pl.BlockSpec(memory_space=pltpu.VMEM)] * (count + 1)
        + [pl.BlockSpec(memory_space=pl.ANY)] * len(kept),
        out_specs=pl.BlockSpec((1, BLOCK, rows), lambda n: (place(n), 0, 0)),
        out_shape=jax.ShapeDtypeStruct((8, BLOCK, rows), F32),
        input_output_aliases={count + 1: 0} if kept else {},
        compiler_params=pltpu.CompilerParams(vmem_limit_bytes=28 * 2**20),
        cost_estimate=pl.CostEstimate(
            flops=2 * count * BLOCK * depth * rows, bytes_accessed=count * BLOCK * (2 * depth + 4 * rows), transcendentals=0
        ),
    )(*[blocks[p] for p in places], normed, *kept)


def state_kernel(at_ref, projected_ref, out_ref):
    core, my_x, my_z = at_ref[0], at_ref[1], at_ref[2]
    columns = projected_ref.shape[-1]
    contract = (((1,), (1,)), ((), ()))
    head = lax.broadcasted_iota(jnp.int32, (HS, 128), 1) // HS

    def rows(first_third, group):
        out = []
        for third, start, stop in pieces(group):
            x, z, c = KV_AT[first_third + third]
            dx, dz = (x - my_x) & 3, (z - my_z) & 3
            outer, inner = (dx, dz) if c == 0 else (dz, dx)
            which = core if c == 0 else 1 - core
            out.append(projected_ref[which * 16 + outer * 4 + inner, start:stop, :])
        return jnp.concatenate(out, axis=0)

    out_ref[GROUPS * HS :, :] = jnp.zeros((STATE_ROWS - GROUPS * HS, 128), F32)
    ones = jnp.ones((8, columns), BF16)
    for g in range(GROUPS):
        keys = jnp.maximum(rows(16, g), 0).astype(BF16)
        values = rows(32, g).astype(BF16)
        full = lax.dot_general(keys, values, contract, preferred_element_type=F32)
        state = full[:HS]
        for b in range(1, 4):
            state = jnp.where(head == b, full[b * HS : (b + 1) * HS], state)
        out_ref[g * HS : (g + 1) * HS, :] = state
        norm = lax.dot_general(ones, keys, contract, preferred_element_type=F32)
        out_ref[GROUPS * HS + g : GROUPS * HS + g + 1, :] = norm[:1]


def block_states(at, projected):
    rows = projected.shape[-1]
    return pl.pallas_call(
        state_kernel,
        in_specs=[pl.BlockSpec(memory_space=pltpu.SMEM), pl.BlockSpec(memory_space=pltpu.VMEM)],
        out_specs=pl.BlockSpec(memory_space=pltpu.VMEM),
        out_shape=jax.ShapeDtypeStruct((STATE_ROWS, 128), F32),
        compiler_params=pltpu.CompilerParams(vmem_limit_bytes=28 * 2**20),
        cost_estimate=pl.CostEstimate(flops=2 * 128 * INNER * rows, bytes_accessed=8 * INNER * rows, transcendentals=0),
    )(at, projected.reshape(32, THIRD, rows))


def query_kernel(at_ref, mine_ref, theirs_ref, normed_ref, out_ref):
    core = at_ref[0]

    def run(weights):
        out = jnp.dot(weights[...], normed_ref[...], preferred_element_type=F32)
        out_ref[0] = jnp.maximum(out.astype(BF16), 0).astype(F32)

    @pl.when(core == 0)
    def _():
        run(mine_ref)

    @pl.when(core != 0)
    def _():
        run(theirs_ref)


def project_queries(at, mine, theirs, normed):
    depth, rows = normed.shape
    return pl.pallas_call(
        query_kernel,
        grid_spec=pltpu.PrefetchScalarGridSpec(
            num_scalar_prefetch=1,
            grid=(4,),
            in_specs=[
                pl.BlockSpec((BLOCK, depth), lambda n, at: (jnp.where(at[0] == 0, n, 0), 0)),
                pl.BlockSpec((BLOCK, depth), lambda n, at: (jnp.where(at[0] == 0, 0, n), 0)),
                pl.BlockSpec(memory_space=pltpu.VMEM),
            ],
            out_specs=pl.BlockSpec((1, BLOCK, rows), lambda n, at: (n, 0, 0)),
        ),
        out_shape=jax.ShapeDtypeStruct((4, BLOCK, rows), F32),
        compiler_params=pltpu.CompilerParams(vmem_limit_bytes=28 * 2**20),
        cost_estimate=pl.CostEstimate(
            flops=2 * INNER * depth * rows, bytes_accessed=INNER * (2 * depth + 4 * rows), transcendentals=0
        ),
    )(at, mine, theirs, normed)


def split_dot(a, b):
    high = a.astype(BF16)
    low = (a - high.astype(F32)).astype(BF16)
    return jnp.dot(high, b, preferred_element_type=F32) + jnp.dot(low, b, preferred_element_type=F32)


def out_kernel(at_ref, queries_ref, seen_ref, mine_ref, theirs_ref, ffn_ref, out_ref, wide_ref, attended_ref):
    core = at_ref[0]

    @pl.when(pl.program_id(0) == 0)
    def _():
        same = (
            lax.broadcasted_iota(jnp.int32, (128, 128), 0) // HS
            == lax.broadcasted_iota(jnp.int32, (128, 128), 1) // HS
        )
        for g in range(GROUPS):
            queries = [queries_ref[Q_AT[u], a:b, :] for u, a, b in pieces(g)]
            queries = jnp.concatenate(queries, axis=0).astype(BF16)
            state = seen_ref[g * HS : (g + 1) * HS, :]
            norm = seen_ref[GROUPS * HS + g : GROUPS * HS + g + 1, :]
            state = jnp.where(same, jnp.concatenate([state] * 4, axis=0), 0.0)
            norm = jnp.where(same, jnp.broadcast_to(norm, (128, 128)), 0.0)
            numerator = split_dot(state.T, queries)
            denominator = split_dot(norm, queries) + 1e-06
            result = numerator / denominator
            row = 0
            for t, a, b in pieces(g):
                slot = (t % 4) * 4 + t // 4
                wide_ref[slot * THIRD + a : slot * THIRD + b, :] = result[row : row + b - a]
                row += b - a
        attended_ref[...] = wide_ref[...].astype(BF16)

    def run(weights):
        out = lax.dot_general(
            weights[...], attended_ref[...], (((0,), (0,)), ((), ())), preferred_element_type=F32
        )
        out_ref[...] = (out + ffn_ref[...].astype(F32)).astype(BF16)

    @pl.when(core == 0)
    def _():
        run(theirs_ref)

    @pl.when(core != 0)
    def _():
        run(mine_ref)


def attend_and_mix(at, queries, seen, mine, theirs, ffn):
    depth, rows = ffn.shape
    wide = 512
    return pl.pallas_call(
        out_kernel,
        grid_spec=pltpu.PrefetchScalarGridSpec(
            num_scalar_prefetch=1,
            grid=(pl.cdiv(depth, wide),),
            in_specs=[
                pl.BlockSpec(memory_space=pltpu.VMEM),
                pl.BlockSpec(memory_space=pltpu.VMEM),
                pl.BlockSpec((INNER, wide), lambda n, at: (0, jnp.where(at[0] == 0, 0, n))),
                pl.BlockSpec((INNER, wide), lambda n, at: (0, jnp.where(at[0] == 0, n, 0))),
                pl.BlockSpec((wide, rows), lambda n, at: (n, 0)),
            ],
            out_specs=pl.BlockSpec((wide, rows), lambda n, at: (n, 0)),
            scratch_shapes=[pltpu.VMEM((INNER, rows), F32), pltpu.VMEM((INNER, rows), BF16)],
        ),
        out_shape=jax.ShapeDtypeStruct((depth, rows), BF16),
        compiler_params=pltpu.CompilerParams(vmem_limit_bytes=40 * 2**20),
        cost_estimate=pl.CostEstimate(
            flops=2 * INNER * depth * rows + 8 * 128 * INNER * rows,
            bytes_accessed=INNER * 2 * depth + 4 * depth * rows,
            transcendentals=0,
        ),
    )(at, queries.reshape(16, THIRD, rows), seen, mine, theirs, ffn)


def halves(a, bit):
    size = a.shape[0] // 2
    return lax.dynamic_slice_in_dim(a, bit * size, size, 0), lax.dynamic_slice_in_dim(a, (1 - bit) * size, size, 0)


def swap_bit(a, bit):
    return lax.ppermute(a, "space", [(i, i ^ (1 << bit)) for i in range(8)])


def sum_over_space(state, space):
    part = state.reshape(8, STATE_ROWS // 8, 128)
    for b in range(3):
        keep, give = halves(part, (space >> b) & 1)
        part = keep + swap_bit(give, b)
    return part


def up_to_here(part):
    for step in (1, 2, 4, 8):
        part = part + lax.ppermute(part, "tm", [(t, t + step) for t in range(16 - step)])
    return part


def spread_over_space(part, space):
    for b in (2, 1, 0):
        theirs = swap_bit(part, b)
        low = ((space >> b) & 1) == 0
        part = jnp.where(low, jnp.concatenate([part, theirs]), jnp.concatenate([theirs, part]))
    return part.reshape(STATE_ROWS, 128)


def after_all(*arrays):
    return lax.optimization_barrier(arrays)


def body(tokens, norm_gain, w_qkv, w_out, ffn_cached):
    t, space = lax.axis_index("tm"), lax.axis_index("space")
    core = space & 1
    at = jnp.stack([core, t >> 2, t & 3]).astype(jnp.int32)
    weights = w_qkv.T
    local = lambda j: lax.dynamic_slice_in_dim(weights, THIRD * j, THIRD, 0)

    traded = lax.ppermute(local(jnp.where(t <= 4, 1 + core, 0)), BOTH, trade_pairs())
    own = jnp.where(t <= 4, traded, local(1 + core))
    part_qo = jnp.where(core == 0, jnp.where(t >= 6, traded, weights[:THIRD]), w_out)

    floats = tokens.T.astype(F32)
    root_mean = jnp.sqrt(jnp.mean(floats * floats, axis=0, keepdims=True) + 1e-06)
    normed = (floats / root_mean * norm_gain[:, None]).astype(BF16)
    own, normed = after_all(own, normed)

    before, after = send(own, first_axis(1)), send(own, first_axis(-1))
    far = jnp.concatenate([send(before[:40], first_axis(1)), send(after[40:], first_axis(-1))])
    block = jnp.concatenate([own, after, far, before])
    before, after = send(block, second_axis(1)), send(block, second_axis(-1))
    block_other = other_core(block)
    buffer = project(None, normed, {0: block})
    buffer = project(buffer, normed, {4: block_other})
    before, after, buffer = after_all(before, after, buffer)

    far = jnp.concatenate([send(before[: BLOCK // 2], second_axis(1)), send(after[BLOCK // 2 :], second_axis(-1))])
    before_other, after_other = other_core(before), other_core(after)
    buffer = project(buffer, normed, {1: after, 3: before})
    buffer = project(buffer, normed, {5: after_other, 7: before_other})
    far, buffer = after_all(far, buffer)

    far_other = other_core(far)
    buffer = project(buffer, normed, {2: far})
    buffer = project(buffer, normed, {6: far_other})
    state = block_states(at, buffer)

    part_qo = lax.all_gather(part_qo, BOTH, axis=0, tiled=True, axis_index_groups=along("zx"))
    part_qo, _ = after_all(part_qo, far)
    mine_qo = lax.all_gather(part_qo, BOTH, axis=0, tiled=True, axis_index_groups=along("xz"))

    state = sum_over_space(state, space)
    mine_qo, state = after_all(mine_qo.reshape(16, THIRD, -1), state)
    theirs_qo = other_core(mine_qo).reshape(INNER, -1)
    mine_qo = mine_qo.reshape(INNER, -1)
    queries = project_queries(at, mine_qo, theirs_qo, normed)
    seen = spread_over_space(up_to_here(state), space)
    return attend_and_mix(at, queries, seen, mine_qo, theirs_qo, ffn_cached.T).T


def solution(mesh):
    return jax.shard_map(
        body,
        mesh=mesh,
        in_specs=(
            P(("tm", "space"), None),
            P(),
            P(None, "tm"),
            P("tm", None),
            P(("tm", "space"), None),
        ),
        out_specs=P(("tm", "space"), None),
        check_vma=False,
    )
```

```python
import functools

import jax
import jax.numpy as jnp
from jax import lax
from jax.experimental import pallas as pl
from jax.experimental.pallas import tpu as pltpu
from jax.sharding import PartitionSpec as P

H = 36
HS = 32
INNER = H * HS
GROUPS = INNER // 128
THIRD = 72
BLOCK = 4 * THIRD
PIECE = 2 * THIRD
STATE_ROWS = 320
BOTH = ("tm", "space")
F32 = jnp.float32
BF16 = jnp.bfloat16

FIRST = {2: 6, 3: 7, 4: 8, 1: 9, 0: 10}
SECOND = {0: 12, 1: 13, 2: 14, 3: 15, 4: 11}


def device(x, z, y, c):
    return ((x % 4) * 4 + z % 4) * 8 + y * 2 + c


def everywhere(move):
    pairs = []
    for t in range(16):
        x, z = divmod(t, 4)
        for y in range(4):
            for c in range(2):
                pairs.append((device(x, z, y, c), device(*move(x, z, y, c))))
    return pairs


def trade_pairs():
    pairs = []
    at = lambda t, y, c: t * 8 + y * 2 + c
    for y in range(4):
        for d in range(5):
            a, b = FIRST[d], SECOND[d]
            pairs += [
                (at(d, y, 0), at(a, y, 0)),
                (at(a, y, 0), at(d, y, 0)),
                (at(d, y, 1), at(b, y, 0)),
                (at(b, y, 1), at(d, y, 1)),
            ]
    return pairs


def kv_third(t, c):
    if t <= 4:
        return 3 * (FIRST, SECOND)[c][t]
    return 3 * t + 1 + c


KV_AT = {kv_third(t, c): (t // 4, t % 4, c) for t in range(16) for c in range(2)}


def q_third(t):
    if t <= 5:
        return 3 * t
    for d in range(5):
        if FIRST[d] == t:
            return 3 * d + 1
        if SECOND[d] == t:
            return 3 * d + 2


Q_AT = {q_third(t): t for t in range(16)}


def pieces(group):
    row, end, out = 128 * group, 128 * group + 128, []
    while row < end:
        third = row // THIRD
        stop = min(end, THIRD * (third + 1))
        out.append((third, row - THIRD * third, stop - THIRD * third))
        row = stop
    return out


def send(a, move):
    return lax.ppermute(a, BOTH, everywhere(move))


def first_axis(step):
    return lambda x, z, y, c: (x, z + step, y, c) if c == 0 else (x + step, z, y, c)


def second_axis(step):
    return lambda x, z, y, c: (x + step, z, y, c) if c == 0 else (x, z + step, y, c)


def other_core(a):
    return send(a, lambda x, z, y, c: (x, z, y, 1 - c))


def start_all(copies):
    for copy in copies:
        copy.start()
    return copies


def wait_all(copies):
    for copy in copies:
        copy.wait()


def load_weights(sources, weights_ref, sems):
    return [
        pltpu.make_async_copy(source, weights_ref.at[pl.ds(n * PIECE, PIECE)], sems.at[n])
        for n, source in enumerate(sources)
    ]


def load_by_core(at_ref, first, second, weights_ref, sems, act):
    for core, sources in enumerate((first, second)):

        @pl.when(at_ref[0] == core)
        def _():
            act(load_weights(sources, weights_ref, sems))


def project_kernel(places, *refs):
    sources, normed_ref, out_ref = refs[: len(places)], refs[len(places)], refs[-1]
    weights = jnp.concatenate([source[...] for source in sources], axis=0)
    out = jnp.dot(weights, normed_ref[...], preferred_element_type=F32).astype(BF16)
    for n, place in enumerate(places):
        out_ref[place] = out[n * PIECE : (n + 1) * PIECE]


def query_kernel(places, at_ref, *refs):
    count = len(places)
    mine, theirs, normed_ref = refs[:count], refs[count : 2 * count], refs[2 * count]
    out_ref, weights_ref, sems = refs[-3:]
    load_by_core(at_ref, mine, theirs, weights_ref, sems, start_all)
    load_by_core(at_ref, mine, theirs, weights_ref, sems, wait_all)
    out = jnp.dot(weights_ref[...], normed_ref[...], preferred_element_type=F32)
    out = jnp.maximum(out, 0).astype(BF16)
    for n, place in enumerate(places):
        out_ref[place] = out[n * PIECE : (n + 1) * PIECE]


def project_call(kernel, buffer, size, places, smem, sources, source_space, scratch, normed):
    count = len(places)
    depth, rows = normed.shape
    kept = [] if buffer is None else [buffer]
    vmem = pl.BlockSpec(memory_space=pltpu.VMEM)
    return pl.pallas_call(
        functools.partial(kernel, tuple(places)),
        in_specs=[pl.BlockSpec(memory_space=pltpu.SMEM)] * len(smem)
        + [pl.BlockSpec(memory_space=source_space)] * len(sources)
        + [vmem] * (1 + len(kept)),
        out_specs=vmem,
        out_shape=jax.ShapeDtypeStruct((size, PIECE, rows), BF16),
        input_output_aliases={len(smem) + len(sources) + 1: 0} if kept else {},
        scratch_shapes=scratch,
        compiler_params=pltpu.CompilerParams(vmem_limit_bytes=14 * 2**20),
        cost_estimate=pl.CostEstimate(
            flops=2 * count * PIECE * depth * rows, bytes_accessed=count * PIECE * 2 * (depth + rows), transcendentals=0
        ),
    )(*smem, *sources, normed, *kept)


def project(buffer, normed, places):
    return project_call(project_kernel, buffer, 16, places, [], list(places.values()), pltpu.VMEM, [], normed)


def project_queries(buffer, at, normed, places):
    sources = [mine for mine, _ in places.values()] + [theirs for _, theirs in places.values()]
    count = len(places)
    scratch = [pltpu.VMEM((count * PIECE, normed.shape[0]), BF16), pltpu.SemaphoreType.DMA((count,))]
    return project_call(query_kernel, buffer, 8, places, [at], sources, pl.ANY, scratch, normed)


def state_kernel(at_ref, projected_ref, out_ref):
    core, my_x, my_z = at_ref[0], at_ref[1], at_ref[2]
    columns = projected_ref.shape[-1]
    contract = (((1,), (1,)), ((), ()))
    head = lax.broadcasted_iota(jnp.int32, (HS, 128), 1) // HS

    def rows(first_third, group):
        out = []
        for third, start, stop in pieces(group):
            x, z, c = KV_AT[first_third + third]
            dx, dz = (x - my_x) & 3, (z - my_z) & 3
            outer, inner = (dx, dz) if c == 0 else (dz, dx)
            which = core if c == 0 else 1 - core
            out.append(projected_ref[which * 16 + outer * 4 + inner].astype(F32)[start:stop])
        return jnp.concatenate(out, axis=0)

    out_ref[GROUPS * HS :, :] = jnp.zeros((STATE_ROWS - GROUPS * HS, 128), F32)
    ones = jnp.ones((8, columns), BF16)
    for g in range(GROUPS):
        keys = jnp.maximum(rows(16, g), 0).astype(BF16)
        values = rows(32, g).astype(BF16)
        full = lax.dot_general(keys, values, contract, preferred_element_type=F32)
        state = full[:HS]
        for b in range(1, 4):
            state = jnp.where(head == b, full[b * HS : (b + 1) * HS], state)
        out_ref[g * HS : (g + 1) * HS, :] = state
        norm = lax.dot_general(ones, keys, contract, preferred_element_type=F32)
        out_ref[GROUPS * HS + g : GROUPS * HS + g + 1, :] = norm[:1]


def block_states(at, projected):
    rows = projected.shape[-1]
    vmem = pl.BlockSpec(memory_space=pltpu.VMEM)
    return pl.pallas_call(
        state_kernel,
        in_specs=[pl.BlockSpec(memory_space=pltpu.SMEM), vmem],
        out_specs=vmem,
        out_shape=jax.ShapeDtypeStruct((STATE_ROWS, 128), F32),
        compiler_params=pltpu.CompilerParams(vmem_limit_bytes=14 * 2**20),
        cost_estimate=pl.CostEstimate(flops=2 * 128 * INNER * rows, bytes_accessed=4 * INNER * rows, transcendentals=0),
    )(at, projected.reshape(32, THIRD, rows))


def split(a):
    high = a.astype(BF16)
    return jnp.concatenate([high, (a - high.astype(F32)).astype(BF16)], axis=1)


def out_kernel(at_ref, queries_ref, seen_ref, *refs):
    mine, theirs, (ffn_ref, out_ref) = refs[:8], refs[8:16], refs[16:18]
    thirds_ref, wide_ref, attended_ref, weights_ref, ffn_vmem, out_vmem = refs[18:24]
    query_sems, weight_sems, ffn_sems, out_sems = refs[24:]
    core, my_x, my_z = at_ref[0], at_ref[1], at_ref[2]
    depth = out_ref.shape[0]
    parts = [(first, min(512, depth - first)) for first in range(0, depth, 512)]

    query_copy = pltpu.make_async_copy(queries_ref, thirds_ref, query_sems.at[0])
    query_copy.start()
    load_by_core(at_ref, theirs, mine, weights_ref, weight_sems, start_all)
    ffn_copies = [
        pltpu.make_async_copy(ffn_ref.at[pl.ds(f, size)], ffn_vmem.at[pl.ds(f, size)], ffn_sems.at[n])
        for n, (f, size) in enumerate(parts)
    ]
    for copy in ffn_copies:
        copy.start()

    same = (
        lax.broadcasted_iota(jnp.int32, (128, 128), 0) // HS == lax.broadcasted_iota(jnp.int32, (128, 128), 1) // HS
    )
    query_copy.wait()
    for g in range(GROUPS):
        queries = []
        for u, a, b in pieces(g):
            dx, dz = (Q_AT[u] // 4 - my_x) & 3, (Q_AT[u] % 4 - my_z) & 3
            queries.append(thirds_ref[dx * 4 + dz].astype(F32)[a:b])
        queries = jnp.concatenate(queries, axis=0).astype(BF16)
        state = seen_ref[g * HS : (g + 1) * HS, :]
        norm = seen_ref[GROUPS * HS + g : GROUPS * HS + g + 1, :]
        state = jnp.where(same, jnp.concatenate([state] * 4, axis=0), 0.0)
        norm = jnp.where(same, jnp.broadcast_to(norm, (128, 128)), 0.0)
        both = split(jnp.concatenate([state.T, norm], axis=0))
        both = jnp.dot(both, jnp.concatenate([queries, queries], axis=0), preferred_element_type=F32)
        result = both[:128] / (both[128:] + 1e-06)
        row = 0
        for t, a, b in pieces(g):
            dx, dz = (t // 4 - my_x) & 3, (t % 4 - my_z) & 3
            wide_ref[dz * 4 + dx, a:b, :] = result[row : row + b - a]
            row += b - a
    attended_ref[...] = wide_ref[...].reshape(attended_ref.shape).astype(BF16)

    load_by_core(at_ref, theirs, mine, weights_ref, weight_sems, wait_all)
    out_copies = []
    for n, (f, size) in enumerate(parts):
        out = lax.dot_general(
            weights_ref[:, f : f + size], attended_ref[...], (((0,), (0,)), ((), ())), preferred_element_type=F32
        )
        ffn_copies[n].wait()
        out_vmem[f : f + size, :] = (out + ffn_vmem[f : f + size, :].astype(F32)).astype(BF16)
        copy = pltpu.make_async_copy(out_vmem.at[pl.ds(f, size)], out_ref.at[pl.ds(f, size)], out_sems.at[n])
        copy.start()
        out_copies.append(copy)
    for copy in out_copies:
        copy.wait()


def attend_and_mix(at, queries, seen, mine, theirs, ffn):
    depth, rows = ffn.shape
    vmem, hbm = pl.BlockSpec(memory_space=pltpu.VMEM), pl.BlockSpec(memory_space=pltpu.HBM)
    parts = pl.cdiv(depth, 512)
    return pl.pallas_call(
        out_kernel,
        in_specs=[pl.BlockSpec(memory_space=pltpu.SMEM), hbm, vmem] + [hbm] * 17,
        out_specs=hbm,
        out_shape=jax.ShapeDtypeStruct((depth, rows), BF16),
        scratch_shapes=[
            pltpu.VMEM((16, THIRD, rows), BF16),
            pltpu.VMEM((16, THIRD, rows), F32),
            pltpu.VMEM((INNER, rows), BF16),
            pltpu.VMEM((INNER, depth), BF16),
            pltpu.VMEM((depth, rows), BF16),
            pltpu.VMEM((depth, rows), BF16),
            pltpu.SemaphoreType.DMA((1,)),
            pltpu.SemaphoreType.DMA((8,)),
            pltpu.SemaphoreType.DMA((parts,)),
            pltpu.SemaphoreType.DMA((parts,)),
        ],
        compiler_params=pltpu.CompilerParams(vmem_limit_bytes=40 * 2**20),
        cost_estimate=pl.CostEstimate(
            flops=2 * INNER * depth * rows + 8 * 128 * INNER * rows,
            bytes_accessed=INNER * 2 * depth + 4 * depth * rows,
            transcendentals=0,
        ),
    )(at, queries.reshape(16, THIRD, rows), seen, *mine, *theirs, ffn)


def swap_bit(a, bit):
    return lax.ppermute(a, "space", [(i, i ^ (1 << bit)) for i in range(8)])


def sum_over_bit(part, place, b):
    size = part.shape[0] // 2
    half = lambda start: lax.dynamic_slice(
        part, (start, 0, 0), (size,) + part.shape[1:], allow_negative_indices=False
    )
    return half(place["keep"][b]) + swap_bit(half(place["give"][b]), b)


def up_to_here(part):
    for step in (1, 2, 4, 8):
        part = part + lax.ppermute(part, "tm", [(t, t + step) for t in range(16 - step)])
    return part


def spread_over_space(part, place):
    for b in (2, 1, 0):
        theirs = swap_bit(part, b)
        part = jnp.where(place["low"][b], jnp.concatenate([part, theirs]), jnp.concatenate([theirs, part]))
    return part.reshape(STATE_ROWS, 128)


def after_all(*arrays):
    return lax.optimization_barrier(arrays)


def body(tokens, norm_gain, w_qkv, w_out, ffn_cached):
    t, space = lax.axis_index("tm"), lax.axis_index("space")
    core = space & 1
    at = jnp.stack([core, t >> 2, t & 3]).astype(jnp.int32)
    weights = w_qkv.T
    local = lambda j: lax.dynamic_slice_in_dim(weights, THIRD * j, THIRD, 0)

    traded = lax.ppermute(local(jnp.where(t <= 4, 1 + core, 0)), BOTH, trade_pairs())
    own_kv = jnp.where(t <= 4, traded, local(1 + core))
    own_qo = jnp.where(core == 0, jnp.where(t >= 6, traded, weights[:THIRD]), w_out)
    own = jnp.concatenate([own_kv, own_qo])

    floats = tokens.T.astype(F32)
    root_mean = jnp.sqrt(jnp.mean(floats * floats, axis=0, keepdims=True) + 1e-06)
    normed = (floats / root_mean * norm_gain[:, None]).astype(BF16)
    bits = [(space >> b) & 1 for b in range(3)]
    place = dict(
        keep=[bits[b] * (4 >> b) for b in range(3)],
        give=[(1 - bits[b]) * (4 >> b) for b in range(3)],
        low=[bits[b] == 0 for b in range(3)],
    )
    own, normed, at, place = lax.optimization_barrier((own, normed, at, place))

    before, after = send(own, first_axis(1)), send(own, first_axis(-1))
    far_kv, far_qo = send(before[:THIRD], first_axis(1)), send(after[THIRD:], first_axis(-1))
    low = jnp.concatenate([own[:THIRD], after[:THIRD]])
    high = jnp.concatenate([far_kv, before[:THIRD]])
    low_qo = jnp.concatenate([own[THIRD:], after[THIRD:]])
    high_qo = jnp.concatenate([far_qo, before[THIRD:]])

    before_low, after_low = send(low, second_axis(1)), send(low, second_axis(-1))
    before_high, after_high = send(high, second_axis(1)), send(high, second_axis(-1))
    buffer = project(None, normed, {0: low, 1: high, 8: other_core(low), 9: other_core(high)})
    before_low, after_low, buffer = after_all(before_low, after_low, buffer)
    far_low = send(before_low, second_axis(1))
    other = {10: other_core(after_low), 14: other_core(before_low)}
    buffer = project(buffer, normed, {2: after_low, 6: before_low, **other})
    after_high, before_high, buffer, low_qo, high_qo = after_all(after_high, before_high, buffer, low_qo, high_qo)
    far_high = send(after_high, second_axis(-1))
    other = {11: other_core(after_high), 15: other_core(before_high)}

    before_low, after_high_qo = send(low_qo, second_axis(1)), send(high_qo, second_axis(-1))
    mine = [low_qo, high_qo, None, None, None, None, None, None]
    theirs = [other_core(a) for a in mine[:2]] + [None] * 6
    both = lambda places: {p: (mine[p], theirs[p]) for p in places}
    buffer = project(buffer, normed, {3: after_high, 7: before_high, **other})
    queries = project_queries(None, at, normed, both((0, 1)))
    far_low, far_high, buffer, queries = after_all(far_low, far_high, buffer, queries)
    far_low_other, far_high_other = other_core(far_low), other_core(far_high)
    before_high, after_low = send(high_qo, second_axis(1)), send(low_qo, second_axis(-1))
    buffer = project(buffer, normed, {4: far_low, 5: far_high})
    buffer = project(buffer, normed, {12: far_low_other, 13: far_high_other})

    state = block_states(at, buffer).reshape(8, STATE_ROWS // 8, 128)
    state = sum_over_bit(state, place, 0)
    mine[3], mine[6], state = after_all(after_high_qo, before_low, state)
    mine[4], mine[5] = send(mine[6], second_axis(1)), send(mine[3], second_axis(-1))
    theirs[3], theirs[6] = other_core(mine[3]), other_core(mine[6])
    state = sum_over_bit(state, place, 1)
    mine[2], mine[7], state = after_all(after_low, before_high, state)
    theirs[2], theirs[7] = other_core(mine[2]), other_core(mine[7])
    state = sum_over_bit(state, place, 2)
    queries = project_queries(queries, at, normed, both((3, 6, 2, 7)))
    mine[4], mine[5], state, queries = after_all(mine[4], mine[5], state, queries)
    theirs[4], theirs[5] = other_core(mine[4]), other_core(mine[5])
    queries = project_queries(queries, at, normed, both((4, 5)))
    state = up_to_here(state)
    state, queries = after_all(state, queries)
    seen = spread_over_space(state, place)
    return attend_and_mix(at, queries, seen, mine, theirs, ffn_cached.T).T


def solution(mesh):
    return jax.shard_map(
        body,
        mesh=mesh,
        in_specs=(
            P(("tm", "space"), None),
            P(),
            P(None, "tm"),
            P("tm", None),
            P(("tm", "space"), None),
        ),
        out_specs=P(("tm", "space"), None),
        check_vma=False,
    )
```

```python
import functools

import jax
import jax.numpy as jnp
from jax import lax
from jax.experimental import pallas as pl
from jax.experimental.pallas import tpu as pltpu
from jax.sharding import PartitionSpec as P

H = 36
HS = 32
INNER = H * HS
GROUPS = INNER // 128
THIRD = 72
BLOCK = 4 * THIRD
PIECE = 2 * THIRD
STATE_ROWS = 320
BOTH = ("tm", "space")
F32 = jnp.float32
BF16 = jnp.bfloat16

FIRST = {0: 8, 1: 6, 2: 10, 3: 7, 4: 9}
SECOND = {0: 12, 1: 13, 2: 14, 3: 15, 4: 11}


def device(x, z, y, c):
    return ((x % 4) * 4 + z % 4) * 8 + y * 2 + c


def everywhere(move):
    pairs = []
    for t in range(16):
        x, z = divmod(t, 4)
        for y in range(4):
            for c in range(2):
                pairs.append((device(x, z, y, c), device(*move(x, z, y, c))))
    return pairs


def trade_pairs():
    pairs = []
    at = lambda t, y, c: t * 8 + y * 2 + c
    for y in range(4):
        for d in range(5):
            a, b = FIRST[d], SECOND[d]
            pairs += [
                (at(d, y, 0), at(a, y, 0)),
                (at(a, y, 0), at(d, y, 0)),
                (at(d, y, 1), at(b, y, 0)),
                (at(b, y, 1), at(d, y, 1)),
            ]
    return pairs


def kv_third(t, c):
    if t <= 4:
        return 3 * (FIRST, SECOND)[c][t]
    return 3 * t + 1 + c


KV_AT = {kv_third(t, c): (t // 4, t % 4, c) for t in range(16) for c in range(2)}


def q_third(t):
    if t <= 5:
        return 3 * t
    for d in range(5):
        if FIRST[d] == t:
            return 3 * d + 1
        if SECOND[d] == t:
            return 3 * d + 2


Q_AT = {q_third(t): t for t in range(16)}


def pieces(group):
    row, end, out = 128 * group, 128 * group + 128, []
    while row < end:
        third = row // THIRD
        stop = min(end, THIRD * (third + 1))
        out.append((third, row - THIRD * third, stop - THIRD * third))
        row = stop
    return out


def send(a, move):
    return lax.ppermute(a, BOTH, everywhere(move))


def first_axis(step):
    return lambda x, z, y, c: (x, z + step, y, c) if c == 0 else (x + step, z, y, c)


def second_axis(step):
    return lambda x, z, y, c: (x + step, z, y, c) if c == 0 else (x, z + step, y, c)


def neighbours(a, axis):
    return send(a, axis(1)), send(a, axis(-1))


def forward(before, after, cut, axis):
    return send(before[:cut], axis(1)), send(after[cut:], axis(-1))


def other_core(a):
    return send(a, lambda x, z, y, c: (x, z, y, 1 - c))


def start_all(copies):
    for copy in copies:
        copy.start()


def wait_all(copies):
    for copy in copies:
        copy.wait()


def project_kernel(places, *refs):
    sources, normed_ref, out_ref = refs[: len(places)], refs[len(places)], refs[-1]
    weights = jnp.concatenate([source[...] for source in sources], axis=0)
    out = jnp.dot(weights, normed_ref[...], preferred_element_type=F32).astype(BF16)
    for n, place in enumerate(places):
        out_ref[place] = out[n * PIECE : (n + 1) * PIECE]


def query_kernel(places, at_ref, *refs):
    count = len(places)
    mine, theirs, normed_ref, out_ref = refs[:count], refs[count : 2 * count], refs[2 * count], refs[-1]
    targets = [place + n for place, source in zip(places, mine) for n in range(source.shape[0] // PIECE)]

    def run(sources):
        weights = jnp.concatenate([source[...] for source in sources], axis=0)
        out = jnp.dot(weights, normed_ref[...], preferred_element_type=F32)
        out = jnp.maximum(out, 0).astype(BF16)
        for n, place in enumerate(targets):
            out_ref[place] = out[n * PIECE : (n + 1) * PIECE]

    @pl.when(at_ref[0] == 0)
    def _():
        run(mine)

    @pl.when(at_ref[0] != 0)
    def _():
        run(theirs)


def project_call(kernel, buffer, size, places, smem, sources, weight_rows, normed):
    depth, rows = normed.shape
    kept = [] if buffer is None else [buffer]
    vmem = pl.BlockSpec(memory_space=pltpu.VMEM)
    return pl.pallas_call(
        functools.partial(kernel, tuple(places)),
        in_specs=[pl.BlockSpec(memory_space=pltpu.SMEM)] * len(smem) + [vmem] * (len(sources) + 1 + len(kept)),
        out_specs=vmem,
        out_shape=jax.ShapeDtypeStruct((size, PIECE, rows), BF16),
        input_output_aliases={len(smem) + len(sources) + 1: 0} if kept else {},
        compiler_params=pltpu.CompilerParams(vmem_limit_bytes=14 * 2**20),
        cost_estimate=pl.CostEstimate(
            flops=2 * weight_rows * depth * rows, bytes_accessed=weight_rows * 2 * (depth + rows), transcendentals=0
        ),
    )(*smem, *sources, normed, *kept)


def project(buffer, normed, places):
    return project_call(project_kernel, buffer, 16, places, [], list(places.values()), len(places) * PIECE, normed)


def project_queries(buffer, at, normed, places):
    mine, theirs = [a for a, _ in places.values()], [b for _, b in places.values()]
    weight_rows = sum(a.shape[0] for a in mine)
    return project_call(query_kernel, buffer, 8, places, [at], mine + theirs, weight_rows, normed)


def state_kernel(at_ref, projected_ref, out_ref):
    core, my_x, my_z = at_ref[0], at_ref[1], at_ref[2]
    columns = projected_ref.shape[-1]
    contract = (((1,), (1,)), ((), ()))
    head = lax.broadcasted_iota(jnp.int32, (HS, 128), 1) // HS

    def rows(first_third, group):
        out = []
        for third, start, stop in pieces(group):
            x, z, c = KV_AT[first_third + third]
            dx, dz = (x - my_x) & 3, (z - my_z) & 3
            outer, inner = (dx, dz) if c == 0 else (dz, dx)
            which = core if c == 0 else 1 - core
            out.append(projected_ref[which * 16 + outer * 4 + inner].astype(F32)[start:stop])
        return jnp.concatenate(out, axis=0)

    out_ref[GROUPS * HS :, :] = jnp.zeros((STATE_ROWS - GROUPS * HS, 128), F32)
    ones = jnp.ones((8, columns), BF16)
    for g in range(GROUPS):
        keys = jnp.maximum(rows(16, g), 0).astype(BF16)
        values = rows(32, g).astype(BF16)
        full = lax.dot_general(keys, values, contract, preferred_element_type=F32)
        state = full[:HS]
        for b in range(1, 4):
            state = jnp.where(head == b, full[b * HS : (b + 1) * HS], state)
        out_ref[g * HS : (g + 1) * HS, :] = state
        norm = lax.dot_general(ones, keys, contract, preferred_element_type=F32)
        out_ref[GROUPS * HS + g : GROUPS * HS + g + 1, :] = norm[:1]


def block_states(at, projected):
    rows = projected.shape[-1]
    vmem = pl.BlockSpec(memory_space=pltpu.VMEM)
    return pl.pallas_call(
        state_kernel,
        in_specs=[pl.BlockSpec(memory_space=pltpu.SMEM), vmem],
        out_specs=vmem,
        out_shape=jax.ShapeDtypeStruct((STATE_ROWS, 128), F32),
        compiler_params=pltpu.CompilerParams(vmem_limit_bytes=14 * 2**20),
        cost_estimate=pl.CostEstimate(flops=2 * 128 * INNER * rows, bytes_accessed=4 * INNER * rows, transcendentals=0),
    )(at, projected.reshape(32, THIRD, rows))


def split(a):
    high = a.astype(BF16)
    return jnp.concatenate([high, (a - high.astype(F32)).astype(BF16)], axis=1)


def out_kernel(at_ref, queries_ref, my_seen_ref, their_seen_ref, *refs):
    mine, theirs, (ffn_ref, out_ref) = refs[:5], refs[5:10], refs[10:12]
    seen_ref, wide_ref, attended_ref, ffn_vmem, out_vmem, ffn_sems, out_sems = refs[12:]
    core, my_x, my_z, my_y = (at_ref[i] for i in range(4))
    depth = out_ref.shape[0]
    parts = [(first, min(512, depth - first)) for first in range(0, depth, 512)]

    ffn_copies = [
        pltpu.make_async_copy(ffn_ref.at[pl.ds(f, size)], ffn_vmem.at[pl.ds(f, size)], ffn_sems.at[n])
        for n, (f, size) in enumerate(parts)
    ]
    start_all(ffn_copies)

    same = (
        lax.broadcasted_iota(jnp.int32, (128, 128), 0) // HS == lax.broadcasted_iota(jnp.int32, (128, 128), 1) // HS
    )
    size = STATE_ROWS // 8
    for p in range(4):
        q = (p - my_y) & 3
        for c, refs in enumerate(((my_seen_ref, their_seen_ref), (their_seen_ref, my_seen_ref))):
            row = (4 * c + p) * size
            seen_ref[row : row + size, :] = jnp.where(core == 0, refs[0][q], refs[1][q])
    for g in range(GROUPS):
        queries = []
        for u, a, b in pieces(g):
            dx, dz = (Q_AT[u] // 4 - my_x) & 3, (Q_AT[u] % 4 - my_z) & 3
            queries.append(queries_ref[dx * 4 + dz].astype(F32)[a:b])
        queries = jnp.concatenate(queries, axis=0).astype(BF16)
        state = seen_ref[g * HS : (g + 1) * HS, :]
        norm = seen_ref[GROUPS * HS + g : GROUPS * HS + g + 1, :]
        state = jnp.where(same, jnp.concatenate([state] * 4, axis=0), 0.0)
        norm = jnp.where(same, jnp.broadcast_to(norm, (128, 128)), 0.0)
        both = split(jnp.concatenate([state.T, norm], axis=0))
        both = jnp.dot(both, jnp.concatenate([queries, queries], axis=0), preferred_element_type=F32)
        result = both[:128] / (both[128:] + 1e-06)
        row = 0
        for t, a, b in pieces(g):
            dx, dz = (t // 4 - my_x) & 3, (t % 4 - my_z) & 3
            wide_ref[dz * 4 + dx, a:b, :] = result[row : row + b - a]
            row += b - a
    attended_ref[...] = wide_ref[...].reshape(attended_ref.shape).astype(BF16)

    out_copies = [
        pltpu.make_async_copy(out_vmem.at[pl.ds(f, size)], out_ref.at[pl.ds(f, size)], out_sems.at[n])
        for n, (f, size) in enumerate(parts)
    ]

    def run(blocks):
        for n, (f, size) in enumerate(parts):
            weights = jnp.concatenate([block[:, f : f + size] for block in blocks], axis=0)
            out = lax.dot_general(
                weights, attended_ref[...], (((0,), (0,)), ((), ())), preferred_element_type=F32
            )
            ffn_copies[n].wait()
            out_vmem[f : f + size, :] = (out + ffn_vmem[f : f + size, :].astype(F32)).astype(BF16)
            out_copies[n].start()

    @pl.when(core == 0)
    def _():
        run(theirs)

    @pl.when(core != 0)
    def _():
        run(mine)

    wait_all(out_copies)


def attend_and_mix(at, queries, my_seen, their_seen, mine, theirs, ffn):
    depth, rows = ffn.shape
    vmem, hbm = pl.BlockSpec(memory_space=pltpu.VMEM), pl.BlockSpec(memory_space=pltpu.HBM)
    parts = pl.cdiv(depth, 512)
    return pl.pallas_call(
        out_kernel,
        in_specs=[pl.BlockSpec(memory_space=pltpu.SMEM)] + [vmem] * 13 + [hbm],
        out_specs=hbm,
        out_shape=jax.ShapeDtypeStruct((depth, rows), BF16),
        scratch_shapes=[
            pltpu.VMEM((STATE_ROWS, 128), F32),
            pltpu.VMEM((16, THIRD, rows), F32),
            pltpu.VMEM((INNER, rows), BF16),
            pltpu.VMEM((depth, rows), BF16),
            pltpu.VMEM((depth, rows), BF16),
            pltpu.SemaphoreType.DMA((parts,)),
            pltpu.SemaphoreType.DMA((parts,)),
        ],
        compiler_params=pltpu.CompilerParams(vmem_limit_bytes=30 * 2**20),
        cost_estimate=pl.CostEstimate(
            flops=2 * INNER * depth * rows + 8 * 128 * INNER * rows,
            bytes_accessed=INNER * 2 * depth + 4 * depth * rows,
            transcendentals=0,
        ),
    )(at, queries.reshape(16, THIRD, rows), my_seen, their_seen, *mine, *theirs, ffn)


def along(axis, step, wrap=True):
    move = {
        "x": lambda x, z, y, c: (x + step, z, y, c),
        "y": lambda x, z, y, c: (x, z, (y + step) % 4, c),
        "z": lambda x, z, y, c: (x, z + step, y, c),
    }[axis]
    pairs = everywhere(move)
    if not wrap:
        at = {"x": lambda i: i // 32, "y": lambda i: i // 2 % 4, "z": lambda i: i // 8 % 4}[axis]
        pairs = [(a, b) for a, b in pairs if at(a) + step < 4]
    return pairs


def chunk(a, start, size=1):
    return lax.dynamic_slice(a, (start, 0, 0), (size,) + a.shape[1:], allow_negative_indices=False)


def sum_over_cores(state, place):
    return chunk(state, place["keep"], 4) + other_core(chunk(state, place["give"], 4))


def sum_over_y(part, place):
    total = chunk(part, place["y"][0])
    for d in range(1, 4):
        total = total + lax.ppermute(chunk(part, place["y"][d]), BOTH, along("y", d))
    return total


def sum_over_z(part, place):
    so_far = total = part
    for d in range(1, 4):
        other = lax.ppermute(part, BOTH, along("z", d))
        so_far = so_far + jnp.where(place["z"][d - 1], other, 0.0)
        total = total + other
    return so_far, total


def sum_over_earlier_x(so_far, total):
    for d in range(1, 4):
        so_far = so_far + lax.ppermute(total, BOTH, along("x", d, wrap=False))
    return so_far


def spread(part):
    parts = [part] + [lax.ppermute(part, BOTH, along("y", -q)) for q in range(1, 4)]
    mine = jnp.concatenate(parts)
    return mine, other_core(mine)


def after_all(*arrays):
    return lax.optimization_barrier(arrays)


def body(tokens, norm_gain, w_qkv, w_out, ffn_cached):
    t, space = lax.axis_index("tm"), lax.axis_index("space")
    core = space & 1
    at = jnp.stack([core, t >> 2, t & 3, space >> 1]).astype(jnp.int32)
    weights = w_qkv.T
    local = lambda j: lax.dynamic_slice_in_dim(weights, THIRD * j, THIRD, 0)

    traded = lax.ppermute(local(jnp.where(t <= 4, 1 + core, 0)), BOTH, trade_pairs())
    own_kv = jnp.where(t <= 4, traded, local(1 + core))
    own_qo = jnp.where(core == 0, jnp.where(t >= 6, traded, weights[:THIRD]), w_out)

    floats = tokens.T.astype(F32)
    root_mean = jnp.sqrt(jnp.mean(floats * floats, axis=0, keepdims=True) + 1e-06)
    y = space >> 1
    place = dict(
        keep=core * 4,
        give=(1 - core) * 4,
        y=[(y + d) & 3 for d in range(4)],
        z=[(t & 3) >= d for d in range(1, 4)],
    )
    own = jnp.concatenate([own_kv, own_qo])
    own, root_mean, at, place = lax.optimization_barrier((own, root_mean, at, place))
    normed = (floats / root_mean * norm_gain[:, None]).astype(BF16)

    before, after = neighbours(own, first_axis)
    far_kv, far_qo = forward(before, after, THIRD, first_axis)
    low = jnp.concatenate([own[:THIRD], after[:THIRD]])
    high = jnp.concatenate([far_kv, before[:THIRD]])
    block = jnp.concatenate([own[THIRD:], after[THIRD:], far_qo, before[THIRD:]])

    before_low, after_low = neighbours(low, second_axis)
    before_high, after_high = neighbours(high, second_axis)
    buffer = project(None, normed, {0: low, 1: high, 8: other_core(low), 9: other_core(high)})
    before_low, after_low, buffer = after_all(before_low, after_low, buffer)
    far_low = send(before_low, second_axis(1))
    other = {10: other_core(after_low), 14: other_core(before_low)}
    buffer = project(buffer, normed, {2: after_low, 6: before_low, **other})
    after_high, before_high, buffer, block = after_all(after_high, before_high, buffer, block)
    far_high = send(after_high, second_axis(-1))
    other = {11: other_core(after_high), 15: other_core(before_high)}
    buffer = project(buffer, normed, {3: after_high, 7: before_high, **other})

    before, after = neighbours(block, second_axis)
    block_other = other_core(block)
    queries = project_queries(None, at, normed, {0: (block, block_other)})
    far_low, far_high, buffer, queries = after_all(far_low, far_high, buffer, queries)
    far_low_other, far_high_other = other_core(far_low), other_core(far_high)
    buffer = project(buffer, normed, {4: far_low, 5: far_high})
    buffer = project(buffer, normed, {12: far_low_other, 13: far_high_other})

    state = block_states(at, buffer).reshape(8, STATE_ROWS // 8, 128)
    state = sum_over_y(sum_over_cores(state, place), place)
    before, after, state = after_all(before, after, state)
    far_low, far_high = forward(before, after, PIECE, second_axis)
    so_far, total = sum_over_z(state, place)
    far_low, far_high, so_far, total = after_all(far_low, far_high, so_far, total)
    after_other, before_other = other_core(after), other_core(before)
    state = sum_over_earlier_x(so_far, total)
    after_other, before_other, state = after_all(after_other, before_other, state)
    queries = project_queries(queries, at, normed, {2: (after, after_other), 6: (before, before_other)})
    far_low_other, far_high_other = other_core(far_low), other_core(far_high)
    queries = project_queries(queries, at, normed, {4: (far_low, far_low_other), 5: (far_high, far_high_other)})
    my_seen, their_seen = spread(state)
    mine = [block, after, far_low, far_high, before]
    theirs = [block_other, after_other, far_low_other, far_high_other, before_other]
    return attend_and_mix(at, queries, my_seen, their_seen, mine, theirs, ffn_cached.T).T


def solution(mesh):
    return jax.shard_map(
        body,
        mesh=mesh,
        in_specs=(
            P(("tm", "space"), None),
            P(),
            P(None, "tm"),
            P("tm", None),
            P(("tm", "space"), None),
        ),
        out_specs=P(("tm", "space"), None),
        check_vma=False,
    )
```

```python
import functools

import jax
import jax.numpy as jnp
from jax import lax
from jax.experimental import pallas as pl
from jax.experimental.pallas import tpu as pltpu
from jax.sharding import PartitionSpec as P

H = 36
HS = 32
INNER = H * HS
GROUPS = INNER // 128
THIRD = 72
BLOCK = 4 * THIRD
PIECE = 2 * THIRD
STATE_ROWS = 320
BOTH = ("tm", "space")
F32 = jnp.float32
BF16 = jnp.bfloat16

FIRST = {0: 8, 1: 6, 2: 10, 3: 7, 4: 9}
SECOND = {0: 12, 1: 13, 2: 14, 3: 15, 4: 11}


def device(x, z, y, c):
    return ((x % 4) * 4 + z % 4) * 8 + y * 2 + c


def everywhere(move):
    pairs = []
    for t in range(16):
        x, z = divmod(t, 4)
        for y in range(4):
            for c in range(2):
                pairs.append((device(x, z, y, c), device(*move(x, z, y, c))))
    return pairs


def trade_pairs():
    pairs = []
    at = lambda t, y, c: t * 8 + y * 2 + c
    for y in range(4):
        for d in range(5):
            a, b = FIRST[d], SECOND[d]
            pairs += [
                (at(d, y, 0), at(a, y, 0)),
                (at(a, y, 0), at(d, y, 0)),
                (at(d, y, 1), at(b, y, 0)),
                (at(b, y, 1), at(d, y, 1)),
            ]
    return pairs


def kv_third(t, c):
    if t <= 4:
        return 3 * (FIRST, SECOND)[c][t]
    return 3 * t + 1 + c


KV_AT = {kv_third(t, c): (t // 4, t % 4, c) for t in range(16) for c in range(2)}


def q_third(t):
    if t <= 5:
        return 3 * t
    for d in range(5):
        if FIRST[d] == t:
            return 3 * d + 1
        if SECOND[d] == t:
            return 3 * d + 2


Q_AT = {q_third(t): t for t in range(16)}


def pieces(group):
    row, end, out = 128 * group, 128 * group + 128, []
    while row < end:
        third = row // THIRD
        stop = min(end, THIRD * (third + 1))
        out.append((third, row - THIRD * third, stop - THIRD * third))
        row = stop
    return out


def send(a, move):
    return lax.ppermute(a, BOTH, everywhere(move))


def first_axis(step):
    return lambda x, z, y, c: (x, z + step, y, c) if c == 0 else (x + step, z, y, c)


def second_axis(step):
    return lambda x, z, y, c: (x + step, z, y, c) if c == 0 else (x, z + step, y, c)


def neighbours(a, axis):
    return send(a, axis(1)), send(a, axis(-1))


def forward(before, after, cut, axis):
    return send(before[:cut], axis(1)), send(after[cut:], axis(-1))


def other_core(a):
    return send(a, lambda x, z, y, c: (x, z, y, 1 - c))


def start_all(copies):
    for copy in copies:
        copy.start()


def wait_all(copies):
    for copy in copies:
        copy.wait()


def project_kernel(places, *refs):
    sources, normed_ref, out_ref = refs[: len(places)], refs[len(places)], refs[-1]
    weights = jnp.concatenate([source[...] for source in sources], axis=0)
    out = jnp.dot(weights, normed_ref[...], preferred_element_type=F32).astype(BF16)
    for n, place in enumerate(places):
        out_ref[place] = out[n * PIECE : (n + 1) * PIECE]


def query_kernel(places, at_ref, *refs):
    count = len(places)
    mine, theirs, normed_ref, out_ref = refs[:count], refs[count : 2 * count], refs[2 * count], refs[-1]
    targets = [place + n for place, source in zip(places, mine) for n in range(source.shape[0] // PIECE)]

    def run(sources):
        weights = jnp.concatenate([source[...] for source in sources], axis=0)
        out = jnp.dot(weights, normed_ref[...], preferred_element_type=F32)
        out = jnp.maximum(out, 0).astype(BF16)
        for n, place in enumerate(targets):
            out_ref[place] = out[n * PIECE : (n + 1) * PIECE]

    @pl.when(at_ref[0] == 0)
    def _():
        run(mine)

    @pl.when(at_ref[0] != 0)
    def _():
        run(theirs)


def project_call(kernel, buffer, size, places, smem, sources, weight_rows, normed):
    depth, rows = normed.shape
    kept = [] if buffer is None else [buffer]
    vmem = pl.BlockSpec(memory_space=pltpu.VMEM)
    return pl.pallas_call(
        functools.partial(kernel, tuple(places)),
        in_specs=[pl.BlockSpec(memory_space=pltpu.SMEM)] * len(smem) + [vmem] * (len(sources) + 1 + len(kept)),
        out_specs=vmem,
        out_shape=jax.ShapeDtypeStruct((size, PIECE, rows), BF16),
        input_output_aliases={len(smem) + len(sources) + 1: 0} if kept else {},
        compiler_params=pltpu.CompilerParams(vmem_limit_bytes=14 * 2**20),
        cost_estimate=pl.CostEstimate(
            flops=2 * weight_rows * depth * rows, bytes_accessed=weight_rows * 2 * (depth + rows), transcendentals=0
        ),
    )(*smem, *sources, normed, *kept)


def project(buffer, normed, places):
    return project_call(project_kernel, buffer, 16, places, [], list(places.values()), len(places) * PIECE, normed)


def project_queries(buffer, at, normed, places):
    mine, theirs = [a for a, _ in places.values()], [b for _, b in places.values()]
    weight_rows = sum(a.shape[0] for a in mine)
    return project_call(query_kernel, buffer, 8, places, [at], mine + theirs, weight_rows, normed)


def state_kernel(at_ref, projected_ref, out_ref):
    core, my_x, my_z = at_ref[0], at_ref[1], at_ref[2]
    columns = projected_ref.shape[-1]
    contract = (((1,), (1,)), ((), ()))
    head = lax.broadcasted_iota(jnp.int32, (HS, 128), 1) // HS

    def rows(first_third, group):
        out = []
        for third, start, stop in pieces(group):
            x, z, c = KV_AT[first_third + third]
            dx, dz = (x - my_x) & 3, (z - my_z) & 3
            outer, inner = (dx, dz) if c == 0 else (dz, dx)
            which = core if c == 0 else 1 - core
            out.append(projected_ref[which * 16 + outer * 4 + inner].astype(F32)[start:stop])
        return jnp.concatenate(out, axis=0)

    out_ref[GROUPS * HS :, :] = jnp.zeros((STATE_ROWS - GROUPS * HS, 128), F32)
    ones = jnp.ones((8, columns), BF16)
    for g in range(GROUPS):
        keys = jnp.maximum(rows(16, g), 0).astype(BF16)
        values = rows(32, g).astype(BF16)
        full = lax.dot_general(keys, values, contract, preferred_element_type=F32)
        state = full[:HS]
        for b in range(1, 4):
            state = jnp.where(head == b, full[b * HS : (b + 1) * HS], state)
        out_ref[g * HS : (g + 1) * HS, :] = state
        norm = lax.dot_general(ones, keys, contract, preferred_element_type=F32)
        out_ref[GROUPS * HS + g : GROUPS * HS + g + 1, :] = norm[:1]


def block_states(at, projected):
    rows = projected.shape[-1]
    vmem = pl.BlockSpec(memory_space=pltpu.VMEM)
    return pl.pallas_call(
        state_kernel,
        in_specs=[pl.BlockSpec(memory_space=pltpu.SMEM), vmem],
        out_specs=vmem,
        out_shape=jax.ShapeDtypeStruct((STATE_ROWS, 128), F32),
        compiler_params=pltpu.CompilerParams(vmem_limit_bytes=14 * 2**20),
        cost_estimate=pl.CostEstimate(flops=2 * 128 * INNER * rows, bytes_accessed=4 * INNER * rows, transcendentals=0),
    )(at, projected.reshape(32, THIRD, rows))


def split(a):
    high = a.astype(BF16)
    return jnp.concatenate([high, (a - high.astype(F32)).astype(BF16)], axis=1)


def out_kernel(at_ref, queries_ref, my_seen_ref, their_seen_ref, *refs):
    mine, theirs, (ffn_ref, out_ref) = refs[:5], refs[5:10], refs[10:12]
    seen_ref, wide_ref, attended_ref, ffn_vmem, out_vmem, ffn_sems, out_sems = refs[12:]
    core, my_x, my_z, my_y = (at_ref[i] for i in range(4))
    depth = out_ref.shape[0]
    parts = [(first, min(512, depth - first)) for first in range(0, depth, 512)]

    ffn_copies = [
        pltpu.make_async_copy(ffn_ref.at[pl.ds(f, size)], ffn_vmem.at[pl.ds(f, size)], ffn_sems.at[n])
        for n, (f, size) in enumerate(parts)
    ]
    start_all(ffn_copies)

    same = (
        lax.broadcasted_iota(jnp.int32, (128, 128), 0) // HS == lax.broadcasted_iota(jnp.int32, (128, 128), 1) // HS
    )
    size = STATE_ROWS // 8
    for p in range(4):
        q = (p - my_y) & 3
        for c, refs in enumerate(((my_seen_ref, their_seen_ref), (their_seen_ref, my_seen_ref))):
            row = (4 * c + p) * size
            seen_ref[row : row + size, :] = jnp.where(core == 0, refs[0][q], refs[1][q])
    for g in range(GROUPS):
        queries = []
        for u, a, b in pieces(g):
            dx, dz = (Q_AT[u] // 4 - my_x) & 3, (Q_AT[u] % 4 - my_z) & 3
            queries.append(queries_ref[dx * 4 + dz].astype(F32)[a:b])
        queries = jnp.concatenate(queries, axis=0).astype(BF16)
        state = seen_ref[g * HS : (g + 1) * HS, :]
        norm = seen_ref[GROUPS * HS + g : GROUPS * HS + g + 1, :]
        state = jnp.where(same, jnp.concatenate([state] * 4, axis=0), 0.0)
        norm = jnp.where(same, jnp.broadcast_to(norm, (128, 128)), 0.0)
        both = split(jnp.concatenate([state.T, norm], axis=0))
        both = jnp.dot(both, jnp.concatenate([queries, queries], axis=0), preferred_element_type=F32)
        result = both[:128] / (both[128:] + 1e-06)
        row = 0
        for t, a, b in pieces(g):
            dx, dz = (t // 4 - my_x) & 3, (t % 4 - my_z) & 3
            wide_ref[dz * 4 + dx, a:b, :] = result[row : row + b - a]
            row += b - a
    attended_ref[...] = wide_ref[...].reshape(attended_ref.shape).astype(BF16)

    out_copies = [
        pltpu.make_async_copy(out_vmem.at[pl.ds(f, size)], out_ref.at[pl.ds(f, size)], out_sems.at[n])
        for n, (f, size) in enumerate(parts)
    ]

    wait_all(ffn_copies)

    def run(blocks):
        for n, (f, size) in enumerate(parts):
            weights = jnp.concatenate([block[:, f : f + size] for block in blocks], axis=0)
            out = lax.dot_general(
                weights, attended_ref[...], (((0,), (0,)), ((), ())), preferred_element_type=F32
            )
            out_vmem[f : f + size, :] = (out + ffn_vmem[f : f + size, :].astype(F32)).astype(BF16)
            out_copies[n].start()

    @pl.when(core == 0)
    def _():
        run(theirs)

    @pl.when(core != 0)
    def _():
        run(mine)

    wait_all(out_copies)


def attend_and_mix(at, queries, my_seen, their_seen, mine, theirs, ffn):
    depth, rows = ffn.shape
    vmem, hbm = pl.BlockSpec(memory_space=pltpu.VMEM), pl.BlockSpec(memory_space=pltpu.HBM)
    parts = pl.cdiv(depth, 512)
    return pl.pallas_call(
        out_kernel,
        in_specs=[pl.BlockSpec(memory_space=pltpu.SMEM)] + [vmem] * 13 + [hbm],
        out_specs=hbm,
        out_shape=jax.ShapeDtypeStruct((depth, rows), BF16),
        scratch_shapes=[
            pltpu.VMEM((STATE_ROWS, 128), F32),
            pltpu.VMEM((16, THIRD, rows), F32),
            pltpu.VMEM((INNER, rows), BF16),
            pltpu.VMEM((depth, rows), BF16),
            pltpu.VMEM((depth, rows), BF16),
            pltpu.SemaphoreType.DMA((parts,)),
            pltpu.SemaphoreType.DMA((parts,)),
        ],
        compiler_params=pltpu.CompilerParams(vmem_limit_bytes=30 * 2**20),
        cost_estimate=pl.CostEstimate(
            flops=2 * INNER * depth * rows + 8 * 128 * INNER * rows,
            bytes_accessed=INNER * 2 * depth + 4 * depth * rows,
            transcendentals=0,
        ),
    )(at, queries.reshape(16, THIRD, rows), my_seen, their_seen, *mine, *theirs, ffn)


def along(axis, step, wrap=True):
    move = {
        "x": lambda x, z, y, c: (x + step, z, y, c),
        "y": lambda x, z, y, c: (x, z, (y + step) % 4, c),
        "z": lambda x, z, y, c: (x, z + step, y, c),
    }[axis]
    pairs = everywhere(move)
    if not wrap:
        at = {"x": lambda i: i // 32, "y": lambda i: i // 2 % 4, "z": lambda i: i // 8 % 4}[axis]
        pairs = [(a, b) for a, b in pairs if at(a) + step < 4]
    return pairs


def chunk(a, start, size=1):
    return lax.dynamic_slice(a, (start, 0, 0), (size,) + a.shape[1:], allow_negative_indices=False)


def sum_over_cores(state, place):
    return chunk(state, place["keep"], 4) + other_core(chunk(state, place["give"], 4))


def sum_over_y(part, place):
    total = chunk(part, place["y"][0])
    for d in range(1, 4):
        total = total + lax.ppermute(chunk(part, place["y"][d]), BOTH, along("y", d))
    return total


def sum_over_z(part, place):
    so_far = total = part
    for d in range(1, 4):
        other = lax.ppermute(part, BOTH, along("z", d))
        so_far = so_far + jnp.where(place["z"][d - 1], other, 0.0)
        total = total + other
    return so_far, total


def sum_over_earlier_x(so_far, total):
    for d in range(1, 4):
        so_far = so_far + lax.ppermute(total, BOTH, along("x", d, wrap=False))
    return so_far


def spread(part):
    parts = [part] + [lax.ppermute(part, BOTH, along("y", -q)) for q in range(1, 4)]
    mine = jnp.concatenate(parts)
    return mine, other_core(mine)


def after_all(*arrays):
    return lax.optimization_barrier(arrays)


def body(tokens, norm_gain, w_qkv, w_out, ffn_cached):
    t, space = lax.axis_index("tm"), lax.axis_index("space")
    core = space & 1
    at = jnp.stack([core, t >> 2, t & 3, space >> 1]).astype(jnp.int32)
    weights = w_qkv.T
    local = lambda j: lax.dynamic_slice_in_dim(weights, THIRD * j, THIRD, 0)

    traded = lax.ppermute(local(jnp.where(t <= 4, 1 + core, 0)), BOTH, trade_pairs())
    own_kv = jnp.where(t <= 4, traded, local(1 + core))
    own_qo = jnp.where(core == 0, jnp.where(t >= 6, traded, weights[:THIRD]), w_out)

    floats = tokens.T.astype(F32)
    root_mean = jnp.sqrt(jnp.mean(floats * floats, axis=0, keepdims=True) + 1e-06)
    y = space >> 1
    place = dict(
        keep=core * 4,
        give=(1 - core) * 4,
        y=[(y + d) & 3 for d in range(4)],
        z=[(t & 3) >= d for d in range(1, 4)],
    )
    own = jnp.concatenate([own_kv, own_qo])
    own, root_mean, at, place = lax.optimization_barrier((own, root_mean, at, place))
    normed = (floats / root_mean * norm_gain[:, None]).astype(BF16)

    before, after = neighbours(own, first_axis)
    far_kv, far_qo = forward(before, after, THIRD, first_axis)
    before, after, far_kv, far_qo = after_all(before, after, far_kv, far_qo)
    low = jnp.concatenate([own[:THIRD], after[:THIRD]])
    high = jnp.concatenate([far_kv, before[:THIRD]])
    block = jnp.concatenate([own[THIRD:], after[THIRD:], far_qo, before[THIRD:]])

    before_low, after_low = neighbours(low, second_axis)
    before_high, after_high = neighbours(high, second_axis)
    buffer = project(None, normed, {0: low, 1: high, 8: other_core(low), 9: other_core(high)})
    before_low, after_low, before_high, after_high, buffer, block = after_all(
        before_low, after_low, before_high, after_high, buffer, block
    )
    far_low, far_high = send(before_low, second_axis(1)), send(after_high, second_axis(-1))
    mine = {2: after_low, 6: before_low, 3: after_high, 7: before_high}
    buffer = project(buffer, normed, mine)
    *pieces_in, buffer, block = after_all(*mine.values(), buffer, block)
    buffer = project(buffer, normed, {8 + p: other_core(a) for p, a in zip(mine, pieces_in)})
    far_low, far_high, buffer, block = after_all(far_low, far_high, buffer, block)
    far_low_other, far_high_other = other_core(far_low), other_core(far_high)
    buffer = project(buffer, normed, {4: far_low, 5: far_high})

    before, after = neighbours(block, second_axis)
    buffer = project(buffer, normed, {12: far_low_other, 13: far_high_other})

    state = block_states(at, buffer).reshape(8, STATE_ROWS // 8, 128)
    block_other = other_core(block)
    state = sum_over_cores(state, place)
    block_other, state = after_all(block_other, state)
    queries = project_queries(None, at, normed, {0: (block, block_other)})
    state = sum_over_y(state, place)
    before, after, state, queries = after_all(before, after, state, queries)
    far_low, far_high = forward(before, after, PIECE, second_axis)
    so_far, total = sum_over_z(state, place)
    far_low, far_high, so_far, total = after_all(far_low, far_high, so_far, total)
    after_other, before_other = other_core(after), other_core(before)
    state = sum_over_earlier_x(so_far, total)
    after_other, before_other, state = after_all(after_other, before_other, state)
    queries = project_queries(queries, at, normed, {2: (after, after_other), 6: (before, before_other)})
    far_low_other, far_high_other = other_core(far_low), other_core(far_high)
    queries = project_queries(queries, at, normed, {4: (far_low, far_low_other), 5: (far_high, far_high_other)})
    my_seen, their_seen = spread(state)
    mine = [block, after, far_low, far_high, before]
    theirs = [block_other, after_other, far_low_other, far_high_other, before_other]
    return attend_and_mix(at, queries, my_seen, their_seen, mine, theirs, ffn_cached.T).T


def solution(mesh):
    return jax.shard_map(
        body,
        mesh=mesh,
        in_specs=(
            P(("tm", "space"), None),
            P(),
            P(None, "tm"),
            P("tm", None),
            P(("tm", "space"), None),
        ),
        out_specs=P(("tm", "space"), None),
        check_vma=False,
    )
```
